32 devices in a mesh: dp: 8 (over z, x), tensor: 4 (over y, core).
Axes of the slice: x: 2, y: 2, z: 4, core: 2. Of those that a mesh axis runs over, the one named last changes fastest.
Arguments:
- attention_grads: bfloat16 [8, 1, 512, 2048], P('dp', None, None, 'tensor')
- expert_grads: bfloat16 [8, 1, 2, 512, 4096], P('dp', None, None, None, 'tensor')
- routing_grads: bfloat16 [8, 4, 1, 36, 512], P('dp', 'tensor'), may hold values from -320 to 320
- attention_master: float32 [512, 2048], P('dp', 'tensor'), may hold values from -0.25 to 0.25
- attention_first: float32 [512, 2048], P('dp', 'tensor'), may hold values from -4 to 4
- attention_second: float32 [512, 2048], P('dp', 'tensor'), may hold values from 0.05 to 2
- expert_master: float32 [2, 512, 4096], P(None, 'dp', 'tensor'), may hold values from -0.25 to 0.25
- expert_first: float32 [2, 512, 4096], P(None, 'dp', 'tensor'), may hold values from -4 to 4
- expert_second: float32 [2, 512, 4096], P(None, 'dp', 'tensor'), may hold values from 0.05 to 2
- routing_master: float32 [36, 512], P(None, ('dp', 'tensor')), may hold values from -4 to 4
- routing_first: float32 [36, 512], P(None, ('dp', 'tensor')), may hold values from -4 to 4
- routing_second: float32 [36, 512], P(None, ('dp', 'tensor')), may hold values from 0.05 to 2
- step_count: int32 [1], replicated, may hold values from 1 to 1000
- learn_rate: float32 [1], replicated, may hold values from 0.05 to 0.3
- clip_level: float32 [1], replicated, may hold values from 0.5 to 2
Outputs:
- attention_renewed: float32 [512, 2048], P('dp', 'tensor')
- attention_momentum: float32 [512, 2048], P('dp', 'tensor')
- attention_variance: float32 [512, 2048], P('dp', 'tensor')
- attention_served: bfloat16 [512, 2048], P(None, 'tensor')
- expert_renewed: float32 [2, 512, 4096], P(None, 'dp', 'tensor')
- expert_momentum: float32 [2, 512, 4096], P(None, 'dp', 'tensor')
- expert_variance: float32 [2, 512, 4096], P(None, 'dp', 'tensor')
- expert_served: bfloat16 [2, 512, 4096], P(None, None, 'tensor')
- routing_renewed: float32 [36, 512], P(None, ('dp', 'tensor'))
- routing_momentum: float32 [36, 512], P(None, ('dp', 'tensor'))
- routing_variance: float32 [36, 512], P(None, ('dp', 'tensor'))
- routing_served: bfloat16 [36, 512], replicated
The draws below stay inside these ranges and needn't reach their ends.
Inputs may be any that keep to these rules, and one draw needn't show every extreme that they name: `step_count`: the number of optimizer steps taken, this one included.
All inputs are finite; a program needn't handle non-finite values.
Results may differ from the reference program's by a relative error of at most 0.0004.
Values may be sent and summed in bfloat16 or wider, within the bound.
A program may use at most 64 MiB of HBM per device.

```python
import math
import jax
import jax.numpy as jnp
from jax import lax

D = 512
FF = 2048
EXPERTS = 32
MICRO = 1
EXP_WIN = 2
ROUTE_ROWS = 36
PARAMS = 5261312
N_DP = 8
N_TENSOR = 4


def rough_partials(key, shape):
    key_base, key_row, key_col = jax.random.split(key, 3)
    rows = shape[-2]
    cols = shape[-1]
    row_place = jnp.arange(rows, dtype=jnp.float32) / rows
    col_place = jnp.arange(cols, dtype=jnp.float32) / cols
    row_scale = jnp.power(10.0, row_place) * jnp.exp(jax.random.uniform(key_row, (rows,), jnp.float32, -0.5, 0.5))
    col_scale = jnp.power(3.0, col_place) * jnp.exp(jax.random.uniform(key_col, (cols,), jnp.float32, -0.7, 0.7))
    base = jax.random.normal(key_base, shape, jnp.float32)
    return base * row_scale[:, None] * col_scale[None, :]


def draw_attention_grads(key, part):
    shape = (N_DP, MICRO, D, 4 * D)
    return rough_partials(jax.random.fold_in(key, 11), shape).astype(jnp.bfloat16)


def draw_expert_grads(key, part):
    shape = (N_DP, MICRO, EXP_WIN, D, 2 * FF)
    return rough_partials(jax.random.fold_in(key, 23), shape).astype(jnp.bfloat16)


def strengthened(values, key, source, target, blocks, factor):
    owner, partner = [(jnp.arange(values.shape[position]) // (values.shape[position] // blocks)).reshape([-1 if axis == position else 1 for axis in range(values.ndim)]) for position in (source, target)]
    chosen = jax.random.permutation(key, blocks)[partner]
    strong = (owner == chosen) | (owner == (partner + blocks // 2) % blocks)
    return jnp.where(strong, factor * values, values)


def level_of(rng, dims, cuts, low, high):
    factor_of, own = 1.0, jax.random.fold_in(rng, 6)
    for dim, parts in cuts:
        draws = jnp.exp(jax.random.uniform(jax.random.fold_in(own, dim), (parts,), jnp.float32, low / len(cuts), high / len(cuts)))
        factor_of = factor_of * jnp.repeat(draws, dims[dim] // parts).reshape([-1 if axis == dim else 1 for axis in range(len(dims))])
    return factor_of


def centred(own_key, extent, width, limit, cuts=(), kind=jnp.bfloat16):
    values = width * jax.random.normal(own_key, extent, jnp.float32)
    if cuts:
        values = values * level_of(own_key, extent, cuts, -0.22, 0.18)
    return jnp.clip(values, -limit, limit).astype(kind)


def heavy_noise(rng, extent, deviation, bound, shards, heavy, kind=jnp.bfloat16):
    result = deviation * jax.random.normal(rng, extent, jnp.float32)
    if shards:
        result = result * level_of(rng, extent, shards, -0.22, 0.18)
    return jnp.clip(strengthened(result, jax.random.fold_in(rng, 3), *heavy), -bound, bound).astype(kind)


def setup_inputs(seed: int = 0) -> dict:
    keys = jax.random.split(jax.random.key(seed), 16)
    attention_grads = draw_attention_grads(jax.random.fold_in(keys[15], 71), 0)
    expert_grads = draw_expert_grads(jax.random.fold_in(keys[15], 71), 0)
    routing_grads = heavy_noise(keys[2], (N_DP, N_TENSOR, MICRO, ROUTE_ROWS, D), 40.0, 320.0, ((0, 8), (1, 4)), (0, 4, 8, 2.0))
    attention_master = centred(keys[3], (D, 4 * D), D ** -0.5, 0.25, ((0, 8), (1, 4)), jnp.float32)
    attention_first = centred(keys[4], (D, 4 * D), 0.5, 4.0, ((0, 8), (1, 4)), jnp.float32)
    attention_second = jnp.clip(jnp.exp(math.log(2.0) - 3.6888794 * jax.random.uniform(keys[5], (D, 4 * D), jnp.float32) ** level_of(keys[5], (D, 4 * D), ((0, 8), (1, 4)), -0.2, 0.2)), 0.05, 2.0)
    expert_master = centred(keys[6], (EXP_WIN, D, 2 * FF), D ** -0.5, 0.25, ((1, 8), (2, 4)), jnp.float32)
    expert_first = centred(keys[7], (EXP_WIN, D, 2 * FF), 0.5, 4.0, ((1, 8), (2, 4)), jnp.float32)
    expert_second = jnp.clip(jnp.exp(math.log(2.0) - 3.6888794 * jax.random.uniform(keys[8], (EXP_WIN, D, 2 * FF), jnp.float32) ** level_of(keys[8], (EXP_WIN, D, 2 * FF), ((1, 8), (2, 4)), -0.2, 0.2)), 0.05, 2.0)
    routing_master = centred(keys[9], (ROUTE_ROWS, D), 0.5, 4.0, ((1, 32),), jnp.float32)
    routing_first = centred(keys[10], (ROUTE_ROWS, D), 0.5, 4.0, ((1, 32),), jnp.float32)
    routing_second = jnp.clip(jnp.exp(math.log(2.0) - 3.6888794 * jax.random.uniform(keys[11], (ROUTE_ROWS, D), jnp.float32) ** level_of(keys[11], (ROUTE_ROWS, D), ((1, 32),), -0.2, 0.2)), 0.05, 2.0)
    step_count = jax.random.randint(keys[12], (1,), 1, 1001).astype(jnp.int32)
    learn_rate = jnp.clip(jnp.exp(jax.random.uniform(keys[13], (1,), jnp.float32, math.log(0.05), math.log(0.3))), 0.05, 0.3)
    clip_level = jnp.clip(jnp.exp(jax.random.uniform(keys[14], (1,), jnp.float32, math.log(0.5), math.log(2.0))), 0.5, 2.0)
    return {"attention_grads": attention_grads, "expert_grads": expert_grads, "routing_grads": routing_grads, "attention_master": attention_master, "attention_first": attention_first, "attention_second": attention_second, "expert_master": expert_master, "expert_first": expert_first, "expert_second": expert_second, "routing_master": routing_master, "routing_first": routing_first, "routing_second": routing_second, "step_count": step_count, "learn_rate": learn_rate, "clip_level": clip_level}


BETA_ONE = 0.9
BETA_TWO = 0.999
EPSILON = 1e-08
DECAY = 0.1

def accumulate(grads):

    def add_slice(total, block):
        return (total + lax.optimization_barrier(jnp.sum(block.astype(jnp.float32), axis=0)), None)
    start = jnp.zeros(grads.shape[2:], jnp.float32)
    total, unused = lax.scan(add_slice, start, grads)
    return total

def adam_update(grad_sum, master, first, second, clip, rate, first_fix, second_fix, mask):
    grad = clip * grad_sum
    momentum = BETA_ONE * first + (1.0 - BETA_ONE) * grad
    variance = BETA_TWO * second + (1.0 - BETA_TWO) * grad * grad
    update = momentum / first_fix / (jnp.sqrt(variance / second_fix) + EPSILON) + DECAY * mask * master
    renewed = master - rate * update
    return (renewed, momentum, variance, renewed.astype(jnp.bfloat16))

def reference(attention_grads, expert_grads, routing_grads, attention_master, attention_first, attention_second, expert_master, expert_first, expert_second, routing_master, routing_first, routing_second, step_count, learn_rate, clip_level):
    attention_sum = accumulate(attention_grads)
    expert_sum = accumulate(expert_grads)
    flat_routing = routing_grads.reshape((routing_grads.shape[0] * routing_grads.shape[1],) + routing_grads.shape[2:])
    routing_sum = accumulate(flat_routing)
    squares = jnp.sum(attention_sum * attention_sum) + jnp.sum(expert_sum * expert_sum) + jnp.sum(routing_sum * routing_sum)
    grad_norm = jnp.sqrt(squares)
    clip = jnp.minimum(1.0, clip_level[0] * jnp.sqrt(jnp.float32(PARAMS)) / (grad_norm + 1e-06))
    steps_done = step_count[0].astype(jnp.float32)
    first_fix = 1.0 - jnp.power(jnp.float32(BETA_ONE), steps_done)
    second_fix = 1.0 - jnp.power(jnp.float32(BETA_TWO), steps_done)
    rate = learn_rate[0]
    row_index = jnp.arange(ROUTE_ROWS, dtype=jnp.int32)
    routing_mask = (row_index < EXPERTS).astype(jnp.float32)[:, None]
    attention_out = adam_update(attention_sum, attention_master, attention_first, attention_second, clip, rate, first_fix, second_fix, jnp.float32(1.0))
    expert_out = adam_update(expert_sum, expert_master, expert_first, expert_second, clip, rate, first_fix, second_fix, jnp.float32(1.0))
    routing_out = adam_update(routing_sum, routing_master, routing_first, routing_second, clip, rate, first_fix, second_fix, routing_mask)
    return (attention_out[0], attention_out[1], attention_out[2], attention_out[3], expert_out[0], expert_out[1], expert_out[2], expert_out[3], routing_out[0], routing_out[1], routing_out[2], routing_out[3])
```

```python
import functools
from functools import reduce

import jax
import jax.numpy as jnp
import numpy as np
from jax import lax
from jax.experimental import pallas as pl
from jax.experimental.pallas import tpu as pltpu
from jax.sharding import PartitionSpec as P

EXPERTS = 32
PARAMS = 5261312


BETA_ONE = 0.9
BETA_TWO = 0.999
EPSILON = 1e-08
DECAY = 0.1


def micro_total(blocks):
    return reduce(lambda left, right: left + right, [blocks[0].astype(jnp.float32)])


def adam_update(grad_sum, master, first, second, clip, rate, first_fix, second_fix, mask):
    grad = clip * grad_sum
    momentum = BETA_ONE * first + (1.0 - BETA_ONE) * grad
    variance = BETA_TWO * second + (1.0 - BETA_TWO) * grad * grad
    update = (
        momentum / first_fix / (jnp.sqrt(variance / second_fix) + EPSILON) + DECAY * mask * master
    )
    renewed = master - rate * update
    return (renewed, momentum, variance, renewed.astype(jnp.bfloat16))


def local(
    attention_grads,
    expert_grads,
    routing_grads,
    attention_master,
    attention_first,
    attention_second,
    expert_master,
    expert_first,
    expert_second,
    routing_master,
    routing_first,
    routing_second,
    step_count,
    learn_rate,
    clip_level,
):
    attention_local = attention_grads[0]
    expert_local = expert_grads[0]
    attention_sum = lax.psum_scatter(
        micro_total(attention_local), "dp", scatter_dimension=0, tiled=True
    )
    expert_sum = lax.psum_scatter(micro_total(expert_local), "dp", scatter_dimension=1, tiled=True)
    expert_pieces = [expert_sum[index] for index in range(expert_sum.shape[0])]
    routing_local = micro_total(routing_grads[0, 0])
    routing_sum = lax.psum_scatter(routing_local, ("dp", "tensor"), scatter_dimension=1, tiled=True)
    expert_squares = reduce(
        lambda left, right: left + right, [jnp.sum(piece * piece) for piece in expert_pieces]
    )
    attention_total, expert_total, routing_total = lax.psum(
        (
            jnp.sum(attention_sum * attention_sum),
            expert_squares,
            jnp.sum(routing_sum * routing_sum),
        ),
        ("dp", "tensor"),
    )
    grad_norm = jnp.sqrt(attention_total + expert_total + routing_total)
    clip = jnp.minimum(1.0, clip_level[0] * jnp.sqrt(jnp.float32(PARAMS)) / (grad_norm + 1e-06))
    steps_done = step_count[0].astype(jnp.float32)
    first_fix = 1.0 - jnp.power(jnp.float32(BETA_ONE), steps_done)
    second_fix = 1.0 - jnp.power(jnp.float32(BETA_TWO), steps_done)
    rate = learn_rate[0]
    attention_out = adam_update(
        attention_sum,
        attention_master,
        attention_first,
        attention_second,
        clip,
        rate,
        first_fix,
        second_fix,
        jnp.float32(1.0),
    )
    attention_served = lax.all_gather(attention_out[3], "dp", axis=0, tiled=True)
    expert_sum = jnp.stack(expert_pieces, axis=0)
    expert_out = adam_update(
        expert_sum,
        expert_master,
        expert_first,
        expert_second,
        clip,
        rate,
        first_fix,
        second_fix,
        jnp.float32(1.0),
    )
    expert_renewed, expert_momentum, expert_variance = (expert_out[0], expert_out[1], expert_out[2])
    expert_served = lax.all_gather(expert_out[3], "dp", axis=1, tiled=True)
    row_index = jnp.arange(routing_master.shape[0], dtype=jnp.int32)
    routing_mask = (row_index < EXPERTS).astype(jnp.float32)[:, None]
    routing_out = adam_update(
        routing_sum,
        routing_master,
        routing_first,
        routing_second,
        clip,
        rate,
        first_fix,
        second_fix,
        routing_mask,
    )
    routing_served = lax.all_gather(routing_out[3], ("dp", "tensor"), axis=1, tiled=True)
    return (
        attention_out[0],
        attention_out[1],
        attention_out[2],
        attention_served,
        expert_renewed,
        expert_momentum,
        expert_variance,
        expert_served,
        routing_out[0],
        routing_out[1],
        routing_out[2],
        routing_served,
    )


MESH = pl.DeviceIdType.MESH
F32 = jnp.float32
BF16 = jnp.bfloat16
WIDE = 512


def power(base, steps):
    result = jnp.full((1, 1), 1.0, F32)
    for bit in range(10):
        factor = F32(float(np.float32(base)) ** (2**bit))
        result = result * jnp.where((steps >> bit) & 1 == 1, factor, F32(1.0))
    return result


def ring_kernel(
    n,
    m,
    ag,
    eg,
    rg,
    am,
    af,
    av,
    em,
    ef,
    ev,
    rm,
    rf,
    rv,
    step_ref,
    rate_ref,
    level_ref,
    o_am,
    o_af,
    o_av,
    o_as,
    o_em,
    o_ef,
    o_ev,
    o_es,
    o_rm,
    o_rf,
    o_rv,
    o_rs,
    ga,
    ge,
    st,
    raw_in,
    sum_in,
    stage,
    gsum,
    served,
    squares,
    norm_t,
    norm_d,
    pad,
    route_out,
    route_in,
    route_t,
    serve_t,
    serve_d,
    load_sem,
    rs_send,
    rs_recv,
    ag_send,
    ag_recv,
    norm_sem,
    route_sem,
    out_sem,
):
    d = lax.axis_index("dp")
    t = lax.axis_index("tensor")
    half_n = n // 2
    rows = am.shape[0]
    hr = rows // 2
    wa = am.shape[1]
    ne, _, we = em.shape
    pieces = [(None, 0, wa)] + [(e, wa + e * we, we) for e in range(ne)]
    z, x = d // 2, d % 2
    pos = z + x * (n - 1 - 2 * z)

    def at_pos(p):
        p = (p + 2 * n) % n
        return 2 * p + (p // half_n) * (2 * n - 1 - 4 * p)

    peers = (at_pos(pos + 1), at_pos(pos - 1))
    sign = (1, -1)
    length = [[half_n, half_n - 1], [half_n - 1, half_n]]

    def row0(owner, h):
        return pl.ds(pl.multiple_of(owner * rows + h * hr, hr), hr)

    loads = [
        pltpu.make_async_copy(ag.at[0, 0], ga, load_sem.at[0]),
        pltpu.make_async_copy(eg.at[0, 0], ge, load_sem.at[1]),
    ]
    k = 2
    state_loads = []
    for which, (a, e) in enumerate(((am, em), (af, ef), (av, ev))):
        for e_i, off, cols in pieces:
            src = a if e_i is None else e.at[e_i]
            state_loads.append(
                pltpu.make_async_copy(src, st.at[which, :, off : off + cols], load_sem.at[k])
            )
            k += 1
    for c in loads + state_loads:
        c.start()

    barrier = pltpu.get_barrier_semaphore()
    for k in range(1, n):
        pl.semaphore_signal(barrier, inc=1, device_id=((d + k) % n, t), device_id_type=MESH)
    for k in range(1, m):
        pl.semaphore_signal(barrier, inc=1, device_id=(d, (t + k) % m), device_id_type=MESH)

    rr, rc = rg.shape[-2:]
    own_cols = rc // (n * m)
    blocks = rc // 128
    per_block = 128 // own_cols
    pad[...] = jnp.zeros_like(pad)
    pad[0:rr, :] = rg[0, 0, 0].astype(F32)
    for j in range(blocks):
        route_out[j] = pad[:, j * 128 : (j + 1) * 128].astype(BF16)

    pl.semaphore_wait(barrier, n - 1 + m - 1)

    def remote(src, dst, send, recv, dp, tensor):
        return pltpu.make_async_remote_copy(
            src_ref=src,
            dst_ref=dst,
            send_sem=send,
            recv_sem=recv,
            device_id=(dp, tensor),
            device_id_type=MESH,
        )

    sends = []

    order = [(p, r, h) for p in range(len(pieces)) for h in range(2) for r in range(2)]

    def rs_copy(s, p, r, h):
        e_i, off, cols = pieces[p]
        lane = slice(off, off + cols)
        if s == 1:
            owner = at_pos(pos + sign[r] * length[r][h])
            src = (
                ag.at[0, 0, row0(owner, h), :]
                if e_i is None
                else eg.at[0, 0, e_i, row0(owner, h), :]
            )
            dst = raw_in.at[r, h, :, lane]
        else:
            src = stage.at[r, h, :, lane] if s == 2 else sum_in.at[r, h, s - 3, :, lane]
            dst = sum_in.at[r, h, s - 2, :, lane]
        return remote(src, dst, rs_send.at[s - 1, p, r, h], rs_recv.at[s - 1, p, r, h], peers[r], t)

    def for_tiles(cols, body):
        wide = cols // WIDE

        def step(i, carry):
            body(pl.multiple_of((i // wide) * 16, 16), pl.multiple_of((i % wide) * WIDE, WIDE))
            return carry

        lax.fori_loop(0, (hr // 16) * wide, step, 0)

    def own(p, owner, h, r0, c0):
        e_i = pieces[p][0]
        rws = pl.ds(pl.multiple_of(owner * rows + h * hr + r0, 16), 16)
        cls = pl.ds(c0, WIDE)
        return (ga[rws, cls] if e_i is None else ge[e_i, rws, cls]).astype(F32)

    for item in order:
        c = rs_copy(1, *item)
        c.start()
        sends.append(c)

    def route_copy(k):
        to = (d + k) % n
        src = route_out.at[(to * m * own_cols) // 128]
        return remote(src, route_in.at[k], route_sem.at[0, k], route_sem.at[1, k], to, t)

    for k in range(1, n):
        c = route_copy(k)
        c.start()
        sends.append(c)
    for c in loads:
        c.wait()
    squares[...] = jnp.zeros_like(squares)

    def route_first():
        total = route_out[(d * m * own_cols) // 128].astype(F32)
        for k in range(1, n):
            route_copy(k).wait_recv()
            total = total + route_in[k].astype(F32)
        route_t[0] = total
        for k in range(1, m):
            c = route_second(k)
            c.start()
            sends.append(c)

    def route_second(k):
        return remote(
            route_t.at[0],
            route_t.at[k],
            route_sem.at[2, k],
            route_sem.at[3, k],
            d,
            (t + k) % m,
        )

    for s in range(1, half_n + 1):
        for p, r, h in order:
            if s > length[r][h]:
                continue
            e_i, off, cols = pieces[p]
            rs_copy(s, p, r, h).wait_recv()
            last = s == length[r][h]
            owner = at_pos(pos + sign[r] * (length[r][h] - s))

            def add(r0, c0, s=s, p=p, r=r, h=h, off=off, last=last, owner=owner):
                rws = pl.ds(r0, 16)
                cls = pl.ds(pl.multiple_of(off + c0, WIDE), WIDE)
                if s == 1:
                    got = raw_in[r, h, rws, cls].astype(F32)
                else:
                    got = sum_in[r, h, s - 2, rws, cls]
                if last and s == half_n:
                    total = gsum[h, rws, cls] + got
                    gsum[h, rws, cls] = total
                    sq = total * total
                    sq = sq[0:8] + sq[8:16]
                    acc = squares[...]
                    for b in range(0, WIDE, 128):
                        acc = acc + sq[:, b : b + 128]
                    squares[...] = acc
                    return
                total = own(p, owner, h, r0, c0) + got
                if last:
                    gsum[h, rws, cls] = total
                elif s == 1:
                    stage[r, h, rws, cls] = total
                else:
                    sum_in[r, h, s - 2, rws, cls] = total

            for_tiles(cols, add)
            if not last:
                c = rs_copy(s + 1, p, r, h)
                c.start()
                sends.append(c)
        if s == 1:
            route_first()

        if s == half_n - 1:
            block = route_t[0]
            for k in range(1, m):
                route_second(k).wait_recv()
                block = block + route_t[k]
            place = (d * m + t) % per_block
            route_sum = jnp.zeros((pad.shape[0], own_cols), F32)
            for b in range(per_block):
                hit = (place == b).astype(F32)
                route_sum = route_sum + hit * block[:, b * own_cols : (b + 1) * own_cols]
            route_sq = jnp.sum(route_sum * route_sum, keepdims=True)

    lane = lax.broadcasted_iota(jnp.int32, (8, 128), 1)
    sub = lax.broadcasted_iota(jnp.int32, (8, 128), 0)
    first = ((lane == 0) & (sub == 0)).astype(F32)
    norm_t[t] = squares[...] + first * route_sq

    def norm_copy(level, k):
        if level == 0:
            buf, who, dp, tensor = norm_t, t, d, (t + k) % m
        else:
            buf, who, dp, tensor = norm_d, d, (d + k) % n, t
        return remote(buf.at[who], buf.at[who], norm_sem.at[level, 0, k], norm_sem.at[level, 1, k], dp, tensor)

    def norm_wait(level, k):
        if level == 0:
            buf, who = norm_t, (t + m - k) % m
        else:
            buf, who = norm_d, (d + n - k) % n
        remote(buf.at[who], buf.at[who], norm_sem.at[level, 0, k], norm_sem.at[level, 1, k], d, t).wait_recv()

    for k in range(1, m):
        c = norm_copy(0, k)
        c.start()
        sends.append(c)
    for c in state_loads:
        c.wait()
    for k in range(1, m):
        norm_wait(0, k)
    total = norm_t[0]
    for k in range(1, m):
        total = total + norm_t[k]
    norm_d[d] = total
    for k in range(1, n):
        c = norm_copy(1, k)
        c.start()
        sends.append(c)
    steps = jnp.full((1, 1), step_ref[0], jnp.int32)
    first_fix = 1.0 - power(BETA_ONE, steps)
    second_fix = 1.0 - power(BETA_TWO, steps)
    rate = rate_ref[0]
    for k in range(1, n):
        norm_wait(1, k)
    total = norm_d[0]
    for k in range(1, n):
        total = total + norm_d[k]
    grad_norm = jnp.sqrt(jnp.sum(total, keepdims=True))
    level = jnp.full((1, 1), level_ref[0], F32)
    clip = jnp.minimum(1.0, level * F32(np.sqrt(np.float32(PARAMS))) / (grad_norm + 1e-06))

    def renew(total, master, first_moment, second_moment, mask):
        grad = clip * total
        momentum = BETA_ONE * first_moment + (1.0 - BETA_ONE) * grad
        variance = BETA_TWO * second_moment + (1.0 - BETA_TWO) * grad * grad
        update = (
            momentum / first_fix / (jnp.sqrt(variance / second_fix) + EPSILON)
            + DECAY * mask * master
        )
        return master - rate * update, momentum, variance

    def out_rows(p, owner, h):
        e_i = pieces[p][0]
        return o_as.at[row0(owner, h), :] if e_i is None else o_es.at[e_i, row0(owner, h), :]

    def ag_copy(s, p, r, h):
        e_i, off, cols = pieces[p]
        owner = at_pos(pos - sign[r] * (s - 1))
        dst = out_rows(p, owner, h)
        src = served.at[h, :, off : off + cols] if s == 1 else dst
        return remote(src, dst, ag_send.at[s - 1, p, r, h], ag_recv.at[s - 1, p, r, h], peers[r], t)

    def ag_wait(s, p, r, h):
        owner = at_pos(pos - sign[r] * s)
        dst = out_rows(p, owner, h)
        remote(dst, dst, ag_send.at[s - 1, p, r, h], ag_recv.at[s - 1, p, r, h], peers[r], t).wait_recv()

    outs = []
    k = 0
    for p in range(len(pieces)):
        e_i, off, cols = pieces[p]
        for h in range(2):

            def update(r0, c0, h=h, off=off):
                cls = pl.ds(pl.multiple_of(off + c0, WIDE), WIDE)
                rws = pl.ds(pl.multiple_of(h * hr + r0, 16), 16)
                w, mom, var = renew(
                    gsum[h, pl.ds(r0, 16), cls],
                    st[0, rws, cls],
                    st[1, rws, cls],
                    st[2, rws, cls],
                    1.0,
                )
                st[0, rws, cls] = w
                st[1, rws, cls] = mom
                st[2, rws, cls] = var
                served[h, pl.ds(r0, 16), cls] = w.astype(BF16)

            for_tiles(cols, update)
            for r in range(2):
                c = ag_copy(1, p, r, h)
                c.start()
                sends.append(c)
            c = pltpu.make_async_copy(
                served.at[h, :, off : off + cols], out_rows(p, d, h), out_sem.at[k]
            )
            k += 1
            c.start()
            outs.append(c)
        for which, (a, e) in enumerate(((o_am, o_em), (o_af, o_ef), (o_av, o_ev))):
            dst = a if e_i is None else e.at[e_i]
            c = pltpu.make_async_copy(st.at[which, :, off : off + cols], dst, out_sem.at[k])
            k += 1
            c.start()
            outs.append(c)

    route_sum = route_sum[0:rr]
    row_index = lax.broadcasted_iota(jnp.int32, (rr, own_cols), 0)
    mask = (row_index < EXPERTS).astype(F32)
    w, mom, var = renew(route_sum, rm[...], rf[...], rv[...], mask)
    o_rm[...] = w
    o_rf[...] = mom
    o_rv[...] = var
    pad[0:rr, 0:128] = jnp.concatenate(
        [(place == b).astype(F32) * w for b in range(per_block)], axis=1
    )
    pad[rr:, 0:128] = jnp.zeros((pad.shape[0] - rr, 128), F32)
    serve_t[0] = pad[:, 0:128].astype(BF16)

    def serve_copy(k):
        return remote(
            serve_t.at[0], serve_t.at[k], route_sem.at[4, k], route_sem.at[5, k], d, (t + k) % m
        )

    def spread_copy(k):
        return remote(
            serve_d.at[d], serve_d.at[d], route_sem.at[6, k], route_sem.at[7, k], (d + k) % n, t
        )

    def spread_wait(k):
        who = (d + n - k) % n
        remote(
            serve_d.at[who], serve_d.at[who], route_sem.at[6, k], route_sem.at[7, k], d, t
        ).wait_recv()

    for k in range(1, m):
        c = serve_copy(k)
        c.start()
        sends.append(c)

    for s in range(1, half_n + 1):
        for p, r, h in order:
            if s > length[r][h]:
                continue
            ag_wait(s, p, r, h)
            if s < length[r][h]:
                c = ag_copy(s + 1, p, r, h)
                c.start()
                sends.append(c)
        if s == 1:
            block = serve_t[0].astype(F32)
            for k in range(1, m):
                serve_copy(k).wait_recv()
                block = block + serve_t[k].astype(F32)
            serve_d[d] = block.astype(BF16)
            for k in range(1, n):
                c = spread_copy(k)
                c.start()
                sends.append(c)
        if s == half_n - 1:
            for k in range(1, n):
                spread_wait(k)
            each = n // blocks
            parts = []
            for j in range(blocks):
                block = serve_d[j * each].astype(F32)
                for b in range(1, each):
                    block = block + serve_d[j * each + b].astype(F32)
                parts.append(block[0:rr])
            o_rs[...] = jnp.concatenate(parts, axis=1).astype(BF16)

    for c in outs:
        c.wait()
    for c in sends:
        c.wait_send()


def ring_local(mesh, *args):
    n, m = mesh.shape["dp"], mesh.shape["tensor"]
    (ag, eg, rg, am, af, av, em, ef, ev, rm, rf, rv, step, rate, level) = args
    rows, wa = am.shape
    ne, _, we = em.shape
    rr, rc = rg.shape[-2:]
    fits = (
        n % 2 == 0
        and n >= 4
        and rows % 32 == 0
        and wa % WIDE == 0
        and we % WIDE == 0
        and ag.shape[1] == 1
        and eg.shape[1] == 1
        and rg.shape[2] == 1
        and rc % 128 == 0
        and 128 % (rc // (n * m)) == 0
        and n % (rc // 128) == 0
    )
    if not fits:
        return local(*args)
    width = wa + ne * we
    half_n = n // 2
    hr = rows // 2
    pr = -(-rr // 16) * 16
    np_ = 1 + ne
    dma = pltpu.SemaphoreType.DMA
    hbm = pl.BlockSpec(memory_space=pl.ANY)
    vmem = pl.BlockSpec(memory_space=pltpu.VMEM)
    smem = pl.BlockSpec(memory_space=pltpu.SMEM)
    sds = jax.ShapeDtypeStruct
    served_a = sds((n * rows, wa), BF16)
    served_e = sds((ne, n * rows, we), BF16)
    like = lambda a: sds(a.shape, a.dtype)
    return pl.pallas_call(
        functools.partial(ring_kernel, n, m),
        out_shape=(
            like(am),
            like(am),
            like(am),
            served_a,
            like(em),
            like(em),
            like(em),
            served_e,
            like(rm),
            like(rm),
            like(rm),
            sds((rr, rc), BF16),
        ),
        in_specs=[hbm, hbm, vmem] + [hbm] * 6 + [vmem] * 3 + [smem] * 3,
        out_specs=(hbm,) * 8 + (vmem,) * 4,
        scratch_shapes=[
            pltpu.VMEM((n * rows, wa), BF16),
            pltpu.VMEM((ne, n * rows, we), BF16),
            pltpu.VMEM((3, rows, width), F32),
            pltpu.VMEM((2, 2, hr, width), BF16),
            pltpu.VMEM((2, 2, half_n - 1, hr, width), F32),
            pltpu.VMEM((2, 2, hr, width), F32),
            pltpu.VMEM((2, hr, width), F32),
            pltpu.VMEM((2, hr, width), BF16),
            pltpu.VMEM((8, 128), F32),
            pltpu.VMEM((m, 8, 128), F32),
            pltpu.VMEM((n, 8, 128), F32),
            pltpu.VMEM((pr, rc), F32),
            pltpu.VMEM((rc // 128, pr, 128), BF16),
            pltpu.VMEM((n, pr, 128), BF16),
            pltpu.VMEM((m, pr, 128), F32),
            pltpu.VMEM((m, pr, 128), BF16),
            pltpu.VMEM((n, pr, 128), BF16),
            dma((2 + 3 * np_,)),
            dma((half_n, np_, 2, 2)),
            dma((half_n, np_, 2, 2)),
            dma((half_n, np_, 2, 2)),
            dma((half_n, np_, 2, 2)),
            dma((2, 2, max(n, m))),
            dma((8, max(n, m))),
            dma((5 * np_,)),
        ],
        compiler_params=pltpu.CompilerParams(
            collective_id=3, has_side_effects=True, vmem_limit_bytes=40 * 2**20
        ),
    )(*args)


def solution(mesh):
    in_specs = (
        P("dp", None, None, "tensor"),
        P("dp", None, None, None, "tensor"),
        P("dp", "tensor", None, None, None),
        P("dp", "tensor"),
        P("dp", "tensor"),
        P("dp", "tensor"),
        P(None, "dp", "tensor"),
        P(None, "dp", "tensor"),
        P(None, "dp", "tensor"),
        P(None, ("dp", "tensor")),
        P(None, ("dp", "tensor")),
        P(None, ("dp", "tensor")),
        P(),
        P(),
        P(),
    )
    out_specs = (
        P("dp", "tensor"),
        P("dp", "tensor"),
        P("dp", "tensor"),
        P(None, "tensor"),
        P(None, "dp", "tensor"),
        P(None, "dp", "tensor"),
        P(None, "dp", "tensor"),
        P(None, None, "tensor"),
        P(None, ("dp", "tensor")),
        P(None, ("dp", "tensor")),
        P(None, ("dp", "tensor")),
        P(),
    )
    body = functools.partial(ring_local, mesh)
    return jax.shard_map(body, mesh=mesh, in_specs=in_specs, out_specs=out_specs, check_vma=False)
```

```python
import functools
from functools import reduce

import jax
import jax.numpy as jnp
import numpy as np
from jax import lax
from jax.experimental import pallas as pl
from jax.experimental.pallas import tpu as pltpu
from jax.sharding import PartitionSpec as P

EXPERTS = 32
PARAMS = 5261312


BETA_ONE = 0.9
BETA_TWO = 0.999
EPSILON = 1e-08
DECAY = 0.1


def micro_total(blocks):
    return reduce(lambda left, right: left + right, [blocks[0].astype(jnp.float32)])


def adam_update(grad_sum, master, first, second, clip, rate, first_fix, second_fix, mask):
    grad = clip * grad_sum
    momentum = BETA_ONE * first + (1.0 - BETA_ONE) * grad
    variance = BETA_TWO * second + (1.0 - BETA_TWO) * grad * grad
    update = (
        momentum / first_fix / (jnp.sqrt(variance / second_fix) + EPSILON) + DECAY * mask * master
    )
    renewed = master - rate * update
    return (renewed, momentum, variance, renewed.astype(jnp.bfloat16))


def local(
    attention_grads,
    expert_grads,
    routing_grads,
    attention_master,
    attention_first,
    attention_second,
    expert_master,
    expert_first,
    expert_second,
    routing_master,
    routing_first,
    routing_second,
    step_count,
    learn_rate,
    clip_level,
):
    attention_local = attention_grads[0]
    expert_local = expert_grads[0]
    attention_sum = lax.psum_scatter(
        micro_total(attention_local), "dp", scatter_dimension=0, tiled=True
    )
    expert_sum = lax.psum_scatter(micro_total(expert_local), "dp", scatter_dimension=1, tiled=True)
    expert_pieces = [expert_sum[index] for index in range(expert_sum.shape[0])]
    routing_local = micro_total(routing_grads[0, 0])
    routing_sum = lax.psum_scatter(routing_local, ("dp", "tensor"), scatter_dimension=1, tiled=True)
    expert_squares = reduce(
        lambda left, right: left + right, [jnp.sum(piece * piece) for piece in expert_pieces]
    )
    attention_total, expert_total, routing_total = lax.psum(
        (
            jnp.sum(attention_sum * attention_sum),
            expert_squares,
            jnp.sum(routing_sum * routing_sum),
        ),
        ("dp", "tensor"),
    )
    grad_norm = jnp.sqrt(attention_total + expert_total + routing_total)
    clip = jnp.minimum(1.0, clip_level[0] * jnp.sqrt(jnp.float32(PARAMS)) / (grad_norm + 1e-06))
    steps_done = step_count[0].astype(jnp.float32)
    first_fix = 1.0 - jnp.power(jnp.float32(BETA_ONE), steps_done)
    second_fix = 1.0 - jnp.power(jnp.float32(BETA_TWO), steps_done)
    rate = learn_rate[0]
    attention_out = adam_update(
        attention_sum,
        attention_master,
        attention_first,
        attention_second,
        clip,
        rate,
        first_fix,
        second_fix,
        jnp.float32(1.0),
    )
    attention_served = lax.all_gather(attention_out[3], "dp", axis=0, tiled=True)
    expert_sum = jnp.stack(expert_pieces, axis=0)
    expert_out = adam_update(
        expert_sum,
        expert_master,
        expert_first,
        expert_second,
        clip,
        rate,
        first_fix,
        second_fix,
        jnp.float32(1.0),
    )
    expert_renewed, expert_momentum, expert_variance = (expert_out[0], expert_out[1], expert_out[2])
    expert_served = lax.all_gather(expert_out[3], "dp", axis=1, tiled=True)
    row_index = jnp.arange(routing_master.shape[0], dtype=jnp.int32)
    routing_mask = (row_index < EXPERTS).astype(jnp.float32)[:, None]
    routing_out = adam_update(
        routing_sum,
        routing_master,
        routing_first,
        routing_second,
        clip,
        rate,
        first_fix,
        second_fix,
        routing_mask,
    )
    routing_served = lax.all_gather(routing_out[3], ("dp", "tensor"), axis=1, tiled=True)
    return (
        attention_out[0],
        attention_out[1],
        attention_out[2],
        attention_served,
        expert_renewed,
        expert_momentum,
        expert_variance,
        expert_served,
        routing_out[0],
        routing_out[1],
        routing_out[2],
        routing_served,
    )


MESH = pl.DeviceIdType.MESH
F32 = jnp.float32
BF16 = jnp.bfloat16
WIDE = 512


def power(base, steps):
    result = jnp.full((1, 1), 1.0, F32)
    for bit in range(10):
        factor = F32(float(np.float32(base)) ** (2**bit))
        result = result * jnp.where((steps >> bit) & 1 == 1, factor, F32(1.0))
    return result


def ring_kernel(
    n,
    m,
    ag,
    eg,
    rg,
    am,
    af,
    av,
    em,
    ef,
    ev,
    rm,
    rf,
    rv,
    step_ref,
    rate_ref,
    level_ref,
    o_am,
    o_af,
    o_av,
    o_as,
    o_em,
    o_ef,
    o_ev,
    o_es,
    o_rm,
    o_rf,
    o_rv,
    o_rs,
    ga,
    ge,
    st,
    raw_in,
    sum_in,
    stage,
    gsum,
    served,
    squares,
    norm_t,
    norm_d,
    pad,
    square,
    route_out,
    route_in,
    route_t,
    serve_t,
    serve_d,
    load_sem,
    rs_send,
    rs_recv,
    ag_send,
    ag_recv,
    norm_sem,
    route_sem,
    out_sem,
):
    d = lax.axis_index("dp")
    t = lax.axis_index("tensor")
    half_n = n // 2
    rows = am.shape[0]
    hr = rows // 2
    wa = am.shape[1]
    ne, _, we = em.shape
    pieces = [(None, 0, wa)] + [(e, wa + e * we, we) for e in range(ne)]
    z, x = d // 2, d % 2
    pos = z + x * (n - 1 - 2 * z)

    def at_pos(p):
        p = (p + 2 * n) % n
        return 2 * p + (p // half_n) * (2 * n - 1 - 4 * p)

    peers = (at_pos(pos + 1), at_pos(pos - 1))
    sign = (1, -1)
    length = [[half_n, half_n - 1], [half_n - 1, half_n]]

    def row0(owner, h):
        return pl.ds(pl.multiple_of(owner * rows + h * hr, hr), hr)

    loads = [
        pltpu.make_async_copy(ag.at[0, 0], ga, load_sem.at[0]),
        pltpu.make_async_copy(eg.at[0, 0], ge, load_sem.at[1]),
    ]
    k = 2
    state_loads = []
    for which, (a, e) in enumerate(((am, em), (af, ef), (av, ev))):
        for e_i, off, cols in pieces:
            src = a if e_i is None else e.at[e_i]
            state_loads.append(
                pltpu.make_async_copy(src, st.at[which, :, off : off + cols], load_sem.at[k])
            )
            k += 1
    for c in loads + state_loads:
        c.start()

    barrier = pltpu.get_barrier_semaphore()
    for k in range(1, n):
        pl.semaphore_signal(barrier, inc=1, device_id=((d + k) % n, t), device_id_type=MESH)
    for k in range(1, m):
        pl.semaphore_signal(barrier, inc=1, device_id=(d, (t + k) % m), device_id_type=MESH)

    rr, rc = rg.shape[-2:]
    own_cols = rc // (n * m)
    blocks = rc // 128
    per_block = 128 // own_cols
    pad[...] = jnp.zeros_like(pad)
    pad[0:rr, :] = rg[0, 0, 0].astype(F32)
    for j in range(blocks):
        route_out[j] = pad[:, j * 128 : (j + 1) * 128].astype(BF16)

    pl.semaphore_wait(barrier, n - 1 + m - 1)

    def remote(src, dst, send, recv, dp, tensor):
        return pltpu.make_async_remote_copy(
            src_ref=src,
            dst_ref=dst,
            send_sem=send,
            recv_sem=recv,
            device_id=(dp, tensor),
            device_id_type=MESH,
        )

    sends = []

    order = [(p, r, h) for p in range(len(pieces)) for h in range(2) for r in range(2)]

    def rs_copy(s, p, r, h):
        e_i, off, cols = pieces[p]
        lane = slice(off, off + cols)
        if s == 1:
            owner = at_pos(pos + sign[r] * length[r][h])
            src = (
                ag.at[0, 0, row0(owner, h), :]
                if e_i is None
                else eg.at[0, 0, e_i, row0(owner, h), :]
            )
            dst = raw_in.at[r, h, :, lane]
        else:
            src = stage.at[r, h, :, lane] if s == 2 else sum_in.at[r, h, s - 3, :, lane]
            dst = sum_in.at[r, h, s - 2, :, lane]
        return remote(src, dst, rs_send.at[s - 1, p, r, h], rs_recv.at[s - 1, p, r, h], peers[r], t)

    def for_tiles(cols, body):
        wide = cols // WIDE

        def step(i, carry):
            body(pl.multiple_of((i // wide) * 16, 16), pl.multiple_of((i % wide) * WIDE, WIDE))
            return carry

        lax.fori_loop(0, (hr // 16) * wide, step, 0)

    def own(p, owner, h, r0, c0):
        e_i = pieces[p][0]
        rws = pl.ds(pl.multiple_of(owner * rows + h * hr + r0, 16), 16)
        cls = pl.ds(c0, WIDE)
        return (ga[rws, cls] if e_i is None else ge[e_i, rws, cls]).astype(F32)

    for item in order:
        c = rs_copy(1, *item)
        c.start()
        sends.append(c)

    def route_copy(k):
        to = (d + k) % n
        src = route_out.at[(to * m * own_cols) // 128]
        return remote(src, route_in.at[k], route_sem.at[0, k], route_sem.at[1, k], to, t)

    for k in range(1, n):
        c = route_copy(k)
        c.start()
        sends.append(c)
    for c in loads:
        c.wait()
    squares[...] = jnp.zeros_like(squares)
    square[...] = jnp.zeros_like(square)

    def route_first():
        total = route_out[(d * m * own_cols) // 128].astype(F32)
        for k in range(1, n):
            route_copy(k).wait_recv()
            total = total + route_in[k].astype(F32)
        route_t[0] = total
        for k in range(1, m):
            c = route_second(k)
            c.start()
            sends.append(c)

    def route_second(k):
        return remote(
            route_t.at[0],
            route_t.at[k],
            route_sem.at[2, k],
            route_sem.at[3, k],
            d,
            (t + k) % m,
        )

    for s in range(1, half_n + 1):
        for p, r, h in order:
            if s > length[r][h]:
                continue
            e_i, off, cols = pieces[p]
            rs_copy(s, p, r, h).wait_recv()
            last = s == length[r][h]
            owner = at_pos(pos + sign[r] * (length[r][h] - s))

            def add(r0, c0, s=s, p=p, r=r, h=h, off=off, last=last, owner=owner):
                rws = pl.ds(r0, 16)
                cls = pl.ds(pl.multiple_of(off + c0, WIDE), WIDE)
                if s == 1:
                    got = raw_in[r, h, rws, cls].astype(F32)
                else:
                    got = sum_in[r, h, s - 2, rws, cls]
                if last and s == half_n:
                    total = gsum[h, rws, cls] + got
                    gsum[h, rws, cls] = total
                    sq = total * total
                    sq = sq[0:8] + sq[8:16]
                    acc = squares[...]
                    for b in range(0, WIDE, 128):
                        acc = acc + sq[:, b : b + 128]
                    squares[...] = acc
                    return
                total = own(p, owner, h, r0, c0) + got
                if last:
                    gsum[h, rws, cls] = total
                elif s == 1:
                    stage[r, h, rws, cls] = total
                else:
                    sum_in[r, h, s - 2, rws, cls] = total

            for_tiles(cols, add)
            if not last:
                c = rs_copy(s + 1, p, r, h)
                c.start()
                sends.append(c)
        if s == 1:
            route_first()

        if s == half_n - 1:
            block = route_t[0]
            for k in range(1, m):
                route_second(k).wait_recv()
                block = block + route_t[k]
            place = (d * m + t) % per_block
            route_sum = jnp.zeros((pad.shape[0], own_cols), F32)
            for b in range(per_block):
                hit = (place == b).astype(F32)
                route_sum = route_sum + hit * block[:, b * own_cols : (b + 1) * own_cols]
            route_sq = jnp.sum(route_sum * route_sum, keepdims=True)

    lane = lax.broadcasted_iota(jnp.int32, (8, 128), 1)
    sub = lax.broadcasted_iota(jnp.int32, (8, 128), 0)
    first = ((lane == 0) & (sub == 0)).astype(F32)
    norm_t[t] = squares[...] + first * route_sq

    def norm_copy(level, k):
        if level == 0:
            buf, who, dp, tensor = norm_t, t, d, (t + k) % m
        else:
            buf, who, dp, tensor = norm_d, d, (d + k) % n, t
        return remote(buf.at[who], buf.at[who], norm_sem.at[level, 0, k], norm_sem.at[level, 1, k], dp, tensor)

    def norm_wait(level, k):
        if level == 0:
            buf, who = norm_t, (t + m - k) % m
        else:
            buf, who = norm_d, (d + n - k) % n
        remote(buf.at[who], buf.at[who], norm_sem.at[level, 0, k], norm_sem.at[level, 1, k], d, t).wait_recv()

    for k in range(1, m):
        c = norm_copy(0, k)
        c.start()
        sends.append(c)
    for c in state_loads:
        c.wait()
    for k in range(1, m):
        norm_wait(0, k)
    total = norm_t[0]
    for k in range(1, m):
        total = total + norm_t[k]
    norm_d[d] = total
    for k in range(1, n):
        c = norm_copy(1, k)
        c.start()
        sends.append(c)
    steps = jnp.full((1, 1), step_ref[0], jnp.int32)
    first_fix = 1.0 - power(BETA_ONE, steps)
    second_fix = 1.0 - power(BETA_TWO, steps)
    rate = rate_ref[0]
    for k in range(1, n):
        norm_wait(1, k)
    total = norm_d[0]
    for k in range(1, n):
        total = total + norm_d[k]
    grad_norm = jnp.sqrt(jnp.sum(total, keepdims=True))
    level = jnp.full((1, 1), level_ref[0], F32)
    clip = jnp.minimum(1.0, level * F32(np.sqrt(np.float32(PARAMS))) / (grad_norm + 1e-06))

    def renew(total, master, first_moment, second_moment, mask):
        grad = clip * total
        momentum = BETA_ONE * first_moment + (1.0 - BETA_ONE) * grad
        variance = BETA_TWO * second_moment + (1.0 - BETA_TWO) * grad * grad
        update = (
            momentum / first_fix / (jnp.sqrt(variance / second_fix) + EPSILON)
            + DECAY * mask * master
        )
        return master - rate * update, momentum, variance

    def out_rows(p, owner, h):
        e_i = pieces[p][0]
        return o_as.at[row0(owner, h), :] if e_i is None else o_es.at[e_i, row0(owner, h), :]

    def ag_copy(s, p, r, h):
        e_i, off, cols = pieces[p]
        owner = at_pos(pos - sign[r] * (s - 1))
        dst = out_rows(p, owner, h)
        src = served.at[h, :, off : off + cols] if s == 1 else dst
        return remote(src, dst, ag_send.at[s - 1, p, r, h], ag_recv.at[s - 1, p, r, h], peers[r], t)

    def ag_wait(s, p, r, h):
        owner = at_pos(pos - sign[r] * s)
        dst = out_rows(p, owner, h)
        remote(dst, dst, ag_send.at[s - 1, p, r, h], ag_recv.at[s - 1, p, r, h], peers[r], t).wait_recv()

    outs = []
    k = 0
    for p in range(len(pieces)):
        e_i, off, cols = pieces[p]
        for h in range(2):

            def update(r0, c0, h=h, off=off):
                cls = pl.ds(pl.multiple_of(off + c0, WIDE), WIDE)
                rws = pl.ds(pl.multiple_of(h * hr + r0, 16), 16)
                w, mom, var = renew(
                    gsum[h, pl.ds(r0, 16), cls],
                    st[0, rws, cls],
                    st[1, rws, cls],
                    st[2, rws, cls],
                    1.0,
                )
                st[0, rws, cls] = w
                st[1, rws, cls] = mom
                st[2, rws, cls] = var
                served[h, pl.ds(r0, 16), cls] = w.astype(BF16)

            for_tiles(cols, update)
            for r in range(2):
                c = ag_copy(1, p, r, h)
                c.start()
                sends.append(c)
            c = pltpu.make_async_copy(
                served.at[h, :, off : off + cols], out_rows(p, d, h), out_sem.at[k]
            )
            k += 1
            c.start()
            outs.append(c)
        for which, (a, e) in enumerate(((o_am, o_em), (o_af, o_ef), (o_av, o_ev))):
            dst = a if e_i is None else e.at[e_i]
            c = pltpu.make_async_copy(st.at[which, :, off : off + cols], dst, out_sem.at[k])
            k += 1
            c.start()
            outs.append(c)

    square[0 : pad.shape[0], 0:own_cols] = route_sum
    route_sum = jnp.transpose(square[...])[0:own_cols, 0:rr]
    row_index = lax.broadcasted_iota(jnp.int32, (own_cols, rr), 1)
    mask = (row_index < EXPERTS).astype(F32)
    w, mom, var = renew(route_sum, rm[...], rf[...], rv[...], mask)
    square[0:own_cols, 0:rr] = w
    w_rows = jnp.transpose(square[...])[0:rr, 0:own_cols]
    o_rm[...] = w
    o_rf[...] = mom
    o_rv[...] = var
    pad[0:rr, 0:128] = jnp.concatenate(
        [(place == b).astype(F32) * w_rows for b in range(per_block)], axis=1
    )
    pad[rr:, 0:128] = jnp.zeros((pad.shape[0] - rr, 128), F32)
    serve_t[0] = pad[:, 0:128].astype(BF16)

    def serve_copy(k):
        return remote(
            serve_t.at[0], serve_t.at[k], route_sem.at[4, k], route_sem.at[5, k], d, (t + k) % m
        )

    def spread_copy(k):
        return remote(
            serve_d.at[d], serve_d.at[d], route_sem.at[6, k], route_sem.at[7, k], (d + k) % n, t
        )

    def spread_wait(k):
        who = (d + n - k) % n
        remote(
            serve_d.at[who], serve_d.at[who], route_sem.at[6, k], route_sem.at[7, k], d, t
        ).wait_recv()

    for k in range(1, m):
        c = serve_copy(k)
        c.start()
        sends.append(c)

    for s in range(1, half_n + 1):
        for p, r, h in order:
            if s > length[r][h]:
                continue
            ag_wait(s, p, r, h)
            if s < length[r][h]:
                c = ag_copy(s + 1, p, r, h)
                c.start()
                sends.append(c)
        if s == 1:
            block = serve_t[0].astype(F32)
            for k in range(1, m):
                serve_copy(k).wait_recv()
                block = block + serve_t[k].astype(F32)
            serve_d[d] = block.astype(BF16)
            for k in range(1, n):
                c = spread_copy(k)
                c.start()
                sends.append(c)
        if s == half_n - 1:
            for k in range(1, n):
                spread_wait(k)
            each = n // blocks
            parts = []
            for j in range(blocks):
                block = serve_d[j * each].astype(F32)
                for b in range(1, each):
                    block = block + serve_d[j * each + b].astype(F32)
                parts.append(block[0:rr])
            o_rs[...] = jnp.concatenate(parts, axis=1).astype(BF16)

    for c in outs:
        c.wait()
    for c in sends:
        c.wait_send()


def place_kernel(count, *refs):
    ins, outs, sem = refs[:count], refs[count : 2 * count], refs[2 * count]
    copies = [
        pltpu.make_async_copy(src, dst, sem.at[k])
        for k, (src, dst) in enumerate(zip(ins[:-1], outs[:-1]))
    ]
    for c in copies:
        c.start()
    outs[-1][...] = ins[-1][...]
    for c in copies:
        c.wait()


def ring_local(mesh, *args):
    n, m = mesh.shape["dp"], mesh.shape["tensor"]
    (ag, eg, rg, am, af, av, em, ef, ev, rm, rf, rv, step, rate, level) = args
    rows, wa = am.shape
    ne, _, we = em.shape
    rr, rc = rg.shape[-2:]
    fits = (
        n % 2 == 0
        and n >= 4
        and rows % 32 == 0
        and wa % WIDE == 0
        and we % WIDE == 0
        and ag.shape[1] == 1
        and eg.shape[1] == 1
        and rg.shape[2] == 1
        and rc % 128 == 0
        and 128 % (rc // (n * m)) == 0
        and rr <= 112
        and n % (rc // 128) == 0
    )
    if not fits:
        return local(*args)
    width = wa + ne * we
    half_n = n // 2
    hr = rows // 2
    pr = -(-rr // 16) * 16
    np_ = 1 + ne
    dma = pltpu.SemaphoreType.DMA
    hbm = pl.BlockSpec(memory_space=pltpu.HBM)
    anywhere = pl.BlockSpec(memory_space=pl.ANY)
    vmem = pl.BlockSpec(memory_space=pltpu.VMEM)
    smem = pl.BlockSpec(memory_space=pltpu.SMEM)
    sds = jax.ShapeDtypeStruct
    served_a = sds((n * rows, wa), BF16)
    served_e = sds((ne, n * rows, we), BF16)
    like = lambda a: sds(a.shape, a.dtype)
    rm, rf, rv = rm.T, rf.T, rv.T
    results = pl.pallas_call(
        functools.partial(ring_kernel, n, m),
        out_shape=(
            like(am),
            like(am),
            like(am),
            served_a,
            like(em),
            like(em),
            like(em),
            served_e,
            like(rm),
            like(rm),
            like(rm),
            sds((rr, rc), BF16),
        ),
        in_specs=[hbm, hbm, vmem] + [hbm] * 6 + [vmem] * 3 + [smem] * 3,
        out_specs=(anywhere,) * 8 + (vmem,) * 4,
        scratch_shapes=[
            pltpu.VMEM((n * rows, wa), BF16),
            pltpu.VMEM((ne, n * rows, we), BF16),
            pltpu.VMEM((3, rows, width), F32),
            pltpu.VMEM((2, 2, hr, width), BF16),
            pltpu.VMEM((2, 2, half_n - 1, hr, width), F32),
            pltpu.VMEM((2, 2, hr, width), F32),
            pltpu.VMEM((2, hr, width), F32),
            pltpu.VMEM((2, hr, width), BF16),
            pltpu.VMEM((8, 128), F32),
            pltpu.VMEM((m, 8, 128), F32),
            pltpu.VMEM((n, 8, 128), F32),
            pltpu.VMEM((pr, rc), F32),
            pltpu.VMEM((128, 128), F32),
            pltpu.VMEM((rc // 128, pr, 128), BF16),
            pltpu.VMEM((n, pr, 128), BF16),
            pltpu.VMEM((m, pr, 128), F32),
            pltpu.VMEM((m, pr, 128), BF16),
            pltpu.VMEM((n, pr, 128), BF16),
            dma((2 + 3 * np_,)),
            dma((half_n, np_, 2, 2)),
            dma((half_n, np_, 2, 2)),
            dma((half_n, np_, 2, 2)),
            dma((half_n, np_, 2, 2)),
            dma((2, 2, max(n, m))),
            dma((8, max(n, m))),
            dma((5 * np_,)),
        ],
        compiler_params=pltpu.CompilerParams(
            collective_id=3, has_side_effects=True, vmem_limit_bytes=62 * 2**20
        ),
    )(ag, eg, rg, am, af, av, em, ef, ev, rm, rf, rv, step, rate, level)
    count = len(results)
    final = pl.pallas_call(
        functools.partial(place_kernel, count),
        out_shape=tuple(like(a) for a in results),
        in_specs=[anywhere] * (count - 1) + [vmem],
        out_specs=(hbm,) * (count - 1) + (vmem,),
        scratch_shapes=[dma((count - 1,))],
        compiler_params=pltpu.CompilerParams(vmem_limit_bytes=62 * 2**20),
    )(*results)
    return final[:8] + (final[8].T, final[9].T, final[10].T, final[11])


def solution(mesh):
    in_specs = (
        P("dp", None, None, "tensor"),
        P("dp", None, None, None, "tensor"),
        P("dp", "tensor", None, None, None),
        P("dp", "tensor"),
        P("dp", "tensor"),
        P("dp", "tensor"),
        P(None, "dp", "tensor"),
        P(None, "dp", "tensor"),
        P(None, "dp", "tensor"),
        P(None, ("dp", "tensor")),
        P(None, ("dp", "tensor")),
        P(None, ("dp", "tensor")),
        P(),
        P(),
        P(),
    )
    out_specs = (
        P("dp", "tensor"),
        P("dp", "tensor"),
        P("dp", "tensor"),
        P(None, "tensor"),
        P(None, "dp", "tensor"),
        P(None, "dp", "tensor"),
        P(None, "dp", "tensor"),
        P(None, None, "tensor"),
        P(None, ("dp", "tensor")),
        P(None, ("dp", "tensor")),
        P(None, ("dp", "tensor")),
        P(),
    )
    body = functools.partial(ring_local, mesh)
    return jax.shard_map(body, mesh=mesh, in_specs=in_specs, out_specs=out_specs, check_vma=False)
```

```python
import functools
from functools import reduce

import jax
import jax.numpy as jnp
import numpy as np
from jax import lax
from jax.experimental import pallas as pl
from jax.experimental.pallas import tpu as pltpu
from jax.sharding import PartitionSpec as P

EXPERTS = 32
PARAMS = 5261312


BETA_ONE = 0.9
BETA_TWO = 0.999
EPSILON = 1e-08
DECAY = 0.1


def micro_total(blocks):
    return reduce(lambda left, right: left + right, [blocks[0].astype(jnp.float32)])


def adam_update(grad_sum, master, first, second, clip, rate, first_fix, second_fix, mask):
    grad = clip * grad_sum
    momentum = BETA_ONE * first + (1.0 - BETA_ONE) * grad
    variance = BETA_TWO * second + (1.0 - BETA_TWO) * grad * grad
    update = (
        momentum / first_fix / (jnp.sqrt(variance / second_fix) + EPSILON) + DECAY * mask * master
    )
    renewed = master - rate * update
    return (renewed, momentum, variance, renewed.astype(jnp.bfloat16))


def local(
    attention_grads,
    expert_grads,
    routing_grads,
    attention_master,
    attention_first,
    attention_second,
    expert_master,
    expert_first,
    expert_second,
    routing_master,
    routing_first,
    routing_second,
    step_count,
    learn_rate,
    clip_level,
):
    attention_local = attention_grads[0]
    expert_local = expert_grads[0]
    attention_sum = lax.psum_scatter(
        micro_total(attention_local), "dp", scatter_dimension=0, tiled=True
    )
    expert_sum = lax.psum_scatter(micro_total(expert_local), "dp", scatter_dimension=1, tiled=True)
    expert_pieces = [expert_sum[index] for index in range(expert_sum.shape[0])]
    routing_local = micro_total(routing_grads[0, 0])
    routing_sum = lax.psum_scatter(routing_local, ("dp", "tensor"), scatter_dimension=1, tiled=True)
    expert_squares = reduce(
        lambda left, right: left + right, [jnp.sum(piece * piece) for piece in expert_pieces]
    )
    attention_total, expert_total, routing_total = lax.psum(
        (
            jnp.sum(attention_sum * attention_sum),
            expert_squares,
            jnp.sum(routing_sum * routing_sum),
        ),
        ("dp", "tensor"),
    )
    grad_norm = jnp.sqrt(attention_total + expert_total + routing_total)
    clip = jnp.minimum(1.0, clip_level[0] * jnp.sqrt(jnp.float32(PARAMS)) / (grad_norm + 1e-06))
    steps_done = step_count[0].astype(jnp.float32)
    first_fix = 1.0 - jnp.power(jnp.float32(BETA_ONE), steps_done)
    second_fix = 1.0 - jnp.power(jnp.float32(BETA_TWO), steps_done)
    rate = learn_rate[0]
    attention_out = adam_update(
        attention_sum,
        attention_master,
        attention_first,
        attention_second,
        clip,
        rate,
        first_fix,
        second_fix,
        jnp.float32(1.0),
    )
    attention_served = lax.all_gather(attention_out[3], "dp", axis=0, tiled=True)
    expert_sum = jnp.stack(expert_pieces, axis=0)
    expert_out = adam_update(
        expert_sum,
        expert_master,
        expert_first,
        expert_second,
        clip,
        rate,
        first_fix,
        second_fix,
        jnp.float32(1.0),
    )
    expert_renewed, expert_momentum, expert_variance = (expert_out[0], expert_out[1], expert_out[2])
    expert_served = lax.all_gather(expert_out[3], "dp", axis=1, tiled=True)
    row_index = jnp.arange(routing_master.shape[0], dtype=jnp.int32)
    routing_mask = (row_index < EXPERTS).astype(jnp.float32)[:, None]
    routing_out = adam_update(
        routing_sum,
        routing_master,
        routing_first,
        routing_second,
        clip,
        rate,
        first_fix,
        second_fix,
        routing_mask,
    )
    routing_served = lax.all_gather(routing_out[3], ("dp", "tensor"), axis=1, tiled=True)
    return (
        attention_out[0],
        attention_out[1],
        attention_out[2],
        attention_served,
        expert_renewed,
        expert_momentum,
        expert_variance,
        expert_served,
        routing_out[0],
        routing_out[1],
        routing_out[2],
        routing_served,
    )


MESH = pl.DeviceIdType.MESH
F32 = jnp.float32
BF16 = jnp.bfloat16
WIDE = 512


def power(base, steps):
    result = jnp.full((1, 1), 1.0, F32)
    for bit in range(10):
        factor = F32(float(np.float32(base)) ** (2**bit))
        result = result * jnp.where((steps >> bit) & 1 == 1, factor, F32(1.0))
    return result


def ring_kernel(
    n,
    m,
    ag,
    eg,
    rg,
    am,
    af,
    av,
    em,
    ef,
    ev,
    rm,
    rf,
    rv,
    step_ref,
    rate_ref,
    level_ref,
    o_am,
    o_af,
    o_av,
    o_as,
    o_em,
    o_ef,
    o_ev,
    o_es,
    o_rm,
    o_rf,
    o_rv,
    o_rs,
    ga,
    ge,
    st,
    raw_in,
    sum_in,
    stage,
    gsum,
    served,
    squares,
    norm_t,
    norm_d,
    pad,
    square,
    route_out,
    route_in,
    route_t,
    serve_t,
    serve_d,
    load_sem,
    rs_send,
    rs_recv,
    ag_send,
    ag_recv,
    norm_sem,
    route_sem,
    out_sem,
):
    d = lax.axis_index("dp")
    t = lax.axis_index("tensor")
    half_n = n // 2
    rows = am.shape[0]
    hr = rows // 2
    wa = am.shape[1]
    ne, _, we = em.shape
    pieces = [(None, 0, wa)] + [(e, wa + e * we, we) for e in range(ne)]
    z, x = d // 2, d % 2
    pos = z + x * (n - 1 - 2 * z)

    def at_pos(p):
        p = (p + 2 * n) % n
        return 2 * p + (p // half_n) * (2 * n - 1 - 4 * p)

    peers = (at_pos(pos + 1), at_pos(pos - 1))
    sign = (1, -1)
    length = [[half_n, half_n - 1], [half_n - 1, half_n]]

    def row0(owner, h):
        return pl.ds(pl.multiple_of(owner * rows + h * hr, hr), hr)

    loads = [
        pltpu.make_async_copy(ag.at[0, 0], ga, load_sem.at[0]),
        pltpu.make_async_copy(eg.at[0, 0], ge, load_sem.at[1]),
    ]
    k = 2
    state_loads = []
    for which, (a, e) in enumerate(((am, em), (af, ef), (av, ev))):
        for e_i, off, cols in pieces:
            src = a if e_i is None else e.at[e_i]
            state_loads.append(
                pltpu.make_async_copy(src, st.at[which, :, off : off + cols], load_sem.at[k])
            )
            k += 1
    for c in loads + state_loads:
        c.start()

    barrier = pltpu.get_barrier_semaphore()
    for k in range(1, n):
        pl.semaphore_signal(barrier, inc=1, device_id=((d + k) % n, t), device_id_type=MESH)
    for k in range(1, m):
        pl.semaphore_signal(barrier, inc=1, device_id=(d, (t + k) % m), device_id_type=MESH)

    rr, rc = rg.shape[-2:]
    own_cols = rc // (n * m)
    blocks = rc // 128
    per_block = 128 // own_cols
    pad[...] = jnp.zeros_like(pad)
    pad[0:rr, :] = rg[0, 0, 0].astype(F32)
    for j in range(blocks):
        route_out[j] = pad[:, j * 128 : (j + 1) * 128].astype(BF16)

    pl.semaphore_wait(barrier, n - 1 + m - 1)

    def remote(src, dst, send, recv, dp, tensor):
        return pltpu.make_async_remote_copy(
            src_ref=src,
            dst_ref=dst,
            send_sem=send,
            recv_sem=recv,
            device_id=(dp, tensor),
            device_id_type=MESH,
        )

    sends = []

    order = [(p, r, h) for p in range(len(pieces)) for h in range(2) for r in range(2)]

    def rs_copy(s, p, r, h):
        e_i, off, cols = pieces[p]
        lane = slice(off, off + cols)
        if s == 1:
            owner = at_pos(pos + sign[r] * length[r][h])
            src = (
                ag.at[0, 0, row0(owner, h), :]
                if e_i is None
                else eg.at[0, 0, e_i, row0(owner, h), :]
            )
            dst = raw_in.at[r, h, :, lane]
        else:
            src = stage.at[r, h, :, lane] if s == 2 else sum_in.at[r, h, s - 3, :, lane]
            dst = sum_in.at[r, h, s - 2, :, lane]
        return remote(src, dst, rs_send.at[s - 1, p, r, h], rs_recv.at[s - 1, p, r, h], peers[r], t)

    def for_tiles(cols, body):
        wide = cols // WIDE

        def step(i, carry):
            body(pl.multiple_of((i // wide) * 16, 16), pl.multiple_of((i % wide) * WIDE, WIDE))
            return carry

        lax.fori_loop(0, (hr // 16) * wide, step, 0)

    def own(p, owner, h, r0, c0):
        e_i = pieces[p][0]
        rws = pl.ds(pl.multiple_of(owner * rows + h * hr + r0, 16), 16)
        cls = pl.ds(c0, WIDE)
        return (ga[rws, cls] if e_i is None else ge[e_i, rws, cls]).astype(F32)

    for item in order:
        c = rs_copy(1, *item)
        c.start()
        sends.append(c)

    def route_copy(k):
        to = (d + k) % n
        src = route_out.at[(to * m * own_cols) // 128]
        return remote(src, route_in.at[k], route_sem.at[0, k], route_sem.at[1, k], to, t)

    for k in range(1, n):
        c = route_copy(k)
        c.start()
        sends.append(c)
    for c in loads:
        c.wait()
    squares[...] = jnp.zeros_like(squares)
    square[...] = jnp.zeros_like(square)

    def route_first():
        total = route_out[(d * m * own_cols) // 128].astype(F32)
        for k in range(1, n):
            route_copy(k).wait_recv()
            total = total + route_in[k].astype(F32)
        route_t[0] = total
        for k in range(1, m):
            c = route_second(k)
            c.start()
            sends.append(c)

    def route_second(k):
        return remote(
            route_t.at[0],
            route_t.at[k],
            route_sem.at[2, k],
            route_sem.at[3, k],
            d,
            (t + k) % m,
        )

    for s in range(1, half_n + 1):
        for p, r, h in order:
            if s > length[r][h]:
                continue
            e_i, off, cols = pieces[p]
            rs_copy(s, p, r, h).wait_recv()
            last = s == length[r][h]
            owner = at_pos(pos + sign[r] * (length[r][h] - s))

            def add(r0, c0, s=s, p=p, r=r, h=h, off=off, last=last, owner=owner):
                rws = pl.ds(r0, 16)
                cls = pl.ds(pl.multiple_of(off + c0, WIDE), WIDE)
                if s == 1:
                    got = raw_in[r, h, rws, cls].astype(F32)
                else:
                    got = sum_in[r, h, s - 2, rws, cls]
                if last and s == half_n:
                    total = gsum[h, rws, cls] + got
                    gsum[h, rws, cls] = total
                    sq = total * total
                    sq = sq[0:8] + sq[8:16]
                    acc = squares[...]
                    for b in range(0, WIDE, 128):
                        acc = acc + sq[:, b : b + 128]
                    squares[...] = acc
                    return
                total = own(p, owner, h, r0, c0) + got
                if last:
                    gsum[h, rws, cls] = total
                elif s == 1:
                    stage[r, h, rws, cls] = total
                else:
                    sum_in[r, h, s - 2, rws, cls] = total

            for_tiles(cols, add)
            if not last:
                c = rs_copy(s + 1, p, r, h)
                c.start()
                sends.append(c)
        if s == 1:
            route_first()

        if s == half_n - 1:
            block = route_t[0]
            for k in range(1, m):
                route_second(k).wait_recv()
                block = block + route_t[k]
            place = (d * m + t) % per_block
            route_sum = jnp.zeros((pad.shape[0], own_cols), F32)
            for b in range(per_block):
                hit = (place == b).astype(F32)
                route_sum = route_sum + hit * block[:, b * own_cols : (b + 1) * own_cols]
            route_sq = jnp.sum(route_sum * route_sum, keepdims=True)

    lane = lax.broadcasted_iota(jnp.int32, (8, 128), 1)
    sub = lax.broadcasted_iota(jnp.int32, (8, 128), 0)
    first = ((lane == 0) & (sub == 0)).astype(F32)
    norm_t[t] = squares[...] + first * route_sq

    def norm_copy(level, k):
        if level == 0:
            buf, who, dp, tensor = norm_t, t, d, (t + k) % m
        else:
            buf, who, dp, tensor = norm_d, d, (d + k) % n, t
        return remote(buf.at[who], buf.at[who], norm_sem.at[level, 0, k], norm_sem.at[level, 1, k], dp, tensor)

    def norm_wait(level, k):
        if level == 0:
            buf, who = norm_t, (t + m - k) % m
        else:
            buf, who = norm_d, (d + n - k) % n
        remote(buf.at[who], buf.at[who], norm_sem.at[level, 0, k], norm_sem.at[level, 1, k], d, t).wait_recv()

    for k in range(1, m):
        c = norm_copy(0, k)
        c.start()
        sends.append(c)
    for c in state_loads:
        c.wait()
    for k in range(1, m):
        norm_wait(0, k)
    total = norm_t[0]
    for k in range(1, m):
        total = total + norm_t[k]
    norm_d[d] = total
    for k in range(1, n):
        c = norm_copy(1, k)
        c.start()
        sends.append(c)
    steps = jnp.full((1, 1), step_ref[0], jnp.int32)
    first_fix = 1.0 - power(BETA_ONE, steps)
    second_fix = 1.0 - power(BETA_TWO, steps)
    rate = rate_ref[0]
    for k in range(1, n):
        norm_wait(1, k)
    total = norm_d[0]
    for k in range(1, n):
        total = total + norm_d[k]
    grad_norm = jnp.sqrt(jnp.sum(total, keepdims=True))
    level = jnp.full((1, 1), level_ref[0], F32)
    clip = jnp.minimum(1.0, level * F32(np.sqrt(np.float32(PARAMS))) / (grad_norm + 1e-06))

    def renew(total, master, first_moment, second_moment, mask):
        grad = clip * total
        momentum = BETA_ONE * first_moment + (1.0 - BETA_ONE) * grad
        variance = BETA_TWO * second_moment + (1.0 - BETA_TWO) * grad * grad
        update = (
            momentum / first_fix / (jnp.sqrt(variance / second_fix) + EPSILON)
            + DECAY * mask * master
        )
        return master - rate * update, momentum, variance

    def out_rows(p, owner, h):
        e_i = pieces[p][0]
        return o_as.at[row0(owner, h), :] if e_i is None else o_es.at[e_i, row0(owner, h), :]

    def ag_copy(s, p, r, h):
        e_i, off, cols = pieces[p]
        owner = at_pos(pos - sign[r] * (s - 1))
        dst = out_rows(p, owner, h)
        src = served.at[h, :, off : off + cols] if s == 1 else dst
        return remote(src, dst, ag_send.at[s - 1, p, r, h], ag_recv.at[s - 1, p, r, h], peers[r], t)

    def ag_wait(s, p, r, h):
        owner = at_pos(pos - sign[r] * s)
        dst = out_rows(p, owner, h)
        remote(dst, dst, ag_send.at[s - 1, p, r, h], ag_recv.at[s - 1, p, r, h], peers[r], t).wait_recv()

    outs = []
    k = 0
    for p in range(len(pieces)):
        e_i, off, cols = pieces[p]
        for h in range(2):

            def update(r0, c0, h=h, off=off):
                cls = pl.ds(pl.multiple_of(off + c0, WIDE), WIDE)
                rws = pl.ds(pl.multiple_of(h * hr + r0, 16), 16)
                w, mom, var = renew(
                    gsum[h, pl.ds(r0, 16), cls],
                    st[0, rws, cls],
                    st[1, rws, cls],
                    st[2, rws, cls],
                    1.0,
                )
                st[0, rws, cls] = w
                st[1, rws, cls] = mom
                st[2, rws, cls] = var
                served[h, pl.ds(r0, 16), cls] = w.astype(BF16)

            for_tiles(cols, update)
            for r in range(2):
                c = ag_copy(1, p, r, h)
                c.start()
                sends.append(c)
            c = pltpu.make_async_copy(
                served.at[h, :, off : off + cols], out_rows(p, d, h), out_sem.at[k]
            )
            k += 1
            c.start()
            outs.append(c)
        for which, (a, e) in enumerate(((o_am, o_em), (o_af, o_ef), (o_av, o_ev))):
            dst = a if e_i is None else e.at[e_i]
            c = pltpu.make_async_copy(st.at[which, :, off : off + cols], dst, out_sem.at[k])
            k += 1
            c.start()
            outs.append(c)

    square[0 : pad.shape[0], 0:own_cols] = route_sum
    route_sum = jnp.transpose(square[...])[0:own_cols, 0:rr]
    row_index = lax.broadcasted_iota(jnp.int32, (own_cols, rr), 1)
    mask = (row_index < EXPERTS).astype(F32)
    w, mom, var = renew(route_sum, rm[...], rf[...], rv[...], mask)
    square[0:own_cols, 0:rr] = w
    w_rows = jnp.transpose(square[...])[0:rr, 0:own_cols]
    o_rm[...] = w
    o_rf[...] = mom
    o_rv[...] = var
    pad[0:rr, 0:128] = jnp.concatenate(
        [(place == b).astype(F32) * w_rows for b in range(per_block)], axis=1
    )
    pad[rr:, 0:128] = jnp.zeros((pad.shape[0] - rr, 128), F32)
    serve_t[0] = pad[:, 0:128].astype(BF16)

    def serve_copy(k):
        return remote(
            serve_t.at[0], serve_t.at[k], route_sem.at[4, k], route_sem.at[5, k], d, (t + k) % m
        )

    def spread_copy(k):
        return remote(
            serve_d.at[d], serve_d.at[d], route_sem.at[6, k], route_sem.at[7, k], (d + k) % n, t
        )

    def spread_wait(k):
        who = (d + n - k) % n
        remote(
            serve_d.at[who], serve_d.at[who], route_sem.at[6, k], route_sem.at[7, k], d, t
        ).wait_recv()

    for k in range(1, m):
        c = serve_copy(k)
        c.start()
        sends.append(c)

    for s in range(1, half_n + 1):
        for p, r, h in order:
            if s > length[r][h]:
                continue
            ag_wait(s, p, r, h)
            if s < length[r][h]:
                c = ag_copy(s + 1, p, r, h)
                c.start()
                sends.append(c)
        if s == 1:
            block = serve_t[0].astype(F32)
            for k in range(1, m):
                serve_copy(k).wait_recv()
                block = block + serve_t[k].astype(F32)
            serve_d[d] = block.astype(BF16)
            for k in range(1, n):
                c = spread_copy(k)
                c.start()
                sends.append(c)
        if s == half_n - 1:
            for k in range(1, n):
                spread_wait(k)
            each = n // blocks
            parts = []
            for j in range(blocks):
                block = serve_d[j * each].astype(F32)
                for b in range(1, each):
                    block = block + serve_d[j * each + b].astype(F32)
                parts.append(block[0:rr])
            o_rs[...] = jnp.concatenate(parts, axis=1).astype(BF16)

    for c in outs:
        c.wait()
    for c in sends:
        c.wait_send()


def place_kernel(count, *refs):
    ins, outs = refs[:count], refs[count : 2 * count]
    held, sem = refs[2 * count : 3 * count - 1], refs[3 * count - 1]
    arrive = [
        pltpu.make_async_copy(ins[k], held[k], sem.at[0, k]) for k in range(count - 1)
    ]
    leave = [
        pltpu.make_async_copy(held[k], outs[k], sem.at[1, k]) for k in range(count - 1)
    ]
    for c in arrive:
        c.start()
    outs[-1][...] = ins[-1][...]
    for a, b in zip(arrive, leave):
        a.wait()
        b.start()
    for c in leave:
        c.wait()


def ring_local(mesh, *args):
    n, m = mesh.shape["dp"], mesh.shape["tensor"]
    (ag, eg, rg, am, af, av, em, ef, ev, rm, rf, rv, step, rate, level) = args
    rows, wa = am.shape
    ne, _, we = em.shape
    rr, rc = rg.shape[-2:]
    fits = (
        n % 2 == 0
        and n >= 4
        and rows % 32 == 0
        and wa % WIDE == 0
        and we % WIDE == 0
        and ag.shape[1] == 1
        and eg.shape[1] == 1
        and rg.shape[2] == 1
        and rc % 128 == 0
        and 128 % (rc // (n * m)) == 0
        and rr <= 112
        and n % (rc // 128) == 0
    )
    if not fits:
        return local(*args)
    width = wa + ne * we
    half_n = n // 2
    hr = rows // 2
    pr = -(-rr // 16) * 16
    np_ = 1 + ne
    dma = pltpu.SemaphoreType.DMA
    hbm = pl.BlockSpec(memory_space=pltpu.HBM)
    anywhere = pl.BlockSpec(memory_space=pl.ANY)
    vmem = pl.BlockSpec(memory_space=pltpu.VMEM)
    smem = pl.BlockSpec(memory_space=pltpu.SMEM)
    sds = jax.ShapeDtypeStruct
    served_a = sds((n * rows, wa), BF16)
    served_e = sds((ne, n * rows, we), BF16)
    like = lambda a: sds(a.shape, a.dtype)
    rm, rf, rv = rm.T, rf.T, rv.T
    results = pl.pallas_call(
        functools.partial(ring_kernel, n, m),
        out_shape=(
            like(am),
            like(am),
            like(am),
            served_a,
            like(em),
            like(em),
            like(em),
            served_e,
            like(rm),
            like(rm),
            like(rm),
            sds((rr, rc), BF16),
        ),
        in_specs=[hbm, hbm, vmem] + [hbm] * 6 + [vmem] * 3 + [smem] * 3,
        out_specs=(anywhere,) * 8 + (vmem,) * 4,
        scratch_shapes=[
            pltpu.VMEM((n * rows, wa), BF16),
            pltpu.VMEM((ne, n * rows, we), BF16),
            pltpu.VMEM((3, rows, width), F32),
            pltpu.VMEM((2, 2, hr, width), BF16),
            pltpu.VMEM((2, 2, half_n - 1, hr, width), F32),
            pltpu.VMEM((2, 2, hr, width), F32),
            pltpu.VMEM((2, hr, width), F32),
            pltpu.VMEM((2, hr, width), BF16),
            pltpu.VMEM((8, 128), F32),
            pltpu.VMEM((m, 8, 128), F32),
            pltpu.VMEM((n, 8, 128), F32),
            pltpu.VMEM((pr, rc), F32),
            pltpu.VMEM((128, 128), F32),
            pltpu.VMEM((rc // 128, pr, 128), BF16),
            pltpu.VMEM((n, pr, 128), BF16),
            pltpu.VMEM((m, pr, 128), F32),
            pltpu.VMEM((m, pr, 128), BF16),
            pltpu.VMEM((n, pr, 128), BF16),
            dma((2 + 3 * np_,)),
            dma((half_n, np_, 2, 2)),
            dma((half_n, np_, 2, 2)),
            dma((half_n, np_, 2, 2)),
            dma((half_n, np_, 2, 2)),
            dma((2, 2, max(n, m))),
            dma((8, max(n, m))),
            dma((5 * np_,)),
        ],
        compiler_params=pltpu.CompilerParams(
            collective_id=3, has_side_effects=True, vmem_limit_bytes=62 * 2**20
        ),
    )(ag, eg, rg, am, af, av, em, ef, ev, rm, rf, rv, step, rate, level)
    count = len(results)
    final = pl.pallas_call(
        functools.partial(place_kernel, count),
        out_shape=tuple(like(a) for a in results),
        in_specs=[anywhere] * (count - 1) + [vmem],
        out_specs=(hbm,) * (count - 1) + (vmem,),
        scratch_shapes=[pltpu.VMEM(a.shape, a.dtype) for a in results[:-1]] + [dma((2, count - 1))],
        compiler_params=pltpu.CompilerParams(vmem_limit_bytes=62 * 2**20),
    )(*results)
    return final[:8] + (final[8].T, final[9].T, final[10].T, final[11])


def solution(mesh):
    in_specs = (
        P("dp", None, None, "tensor"),
        P("dp", None, None, None, "tensor"),
        P("dp", "tensor", None, None, None),
        P("dp", "tensor"),
        P("dp", "tensor"),
        P("dp", "tensor"),
        P(None, "dp", "tensor"),
        P(None, "dp", "tensor"),
        P(None, "dp", "tensor"),
        P(None, ("dp", "tensor")),
        P(None, ("dp", "tensor")),
        P(None, ("dp", "tensor")),
        P(),
        P(),
        P(),
    )
    out_specs = (
        P("dp", "tensor"),
        P("dp", "tensor"),
        P("dp", "tensor"),
        P(None, "tensor"),
        P(None, "dp", "tensor"),
        P(None, "dp", "tensor"),
        P(None, "dp", "tensor"),
        P(None, None, "tensor"),
        P(None, ("dp", "tensor")),
        P(None, ("dp", "tensor")),
        P(None, ("dp", "tensor")),
        P(),
    )
    body = functools.partial(ring_local, mesh)
    return jax.shard_map(body, mesh=mesh, in_specs=in_specs, out_specs=out_specs, check_vma=False)
```
